32 devices in a mesh: seq: 8 (over z, y), ch: 4 (over x, core).
Axes of the slice: x: 2, y: 2, z: 4, core: 2. Of those that a mesh axis runs over, the one named last changes fastest.
Arguments:
- hidden: bfloat16 [3, 8192, 1536], P(None, 'seq'), may hold values from -6 to 6
- gain_in: float32 [1536], replicated, may hold values from 0.5 to 1.5
- in_weight: bfloat16 [1536, 3, 1536], P(None, None, 'ch'), may hold values from -0.15625 to 0.15625
- conv_weight: bfloat16 [3, 1536], P(None, 'ch'), may hold values from -3 to 3
- out_weight: bfloat16 [1536, 1536], P(None, 'ch'), may hold values from -0.15625 to 0.15625
- gain_mid: float32 [1536], replicated, may hold values from 0.5 to 1.5
- gate_up_weight: bfloat16 [1536, 2, 6912], P(None, None, 'ch'), may hold values from -0.15625 to 0.15625
- down_weight: bfloat16 [1536, 6912], P(None, 'ch'), may hold values from -0.078125 to 0.078125
- cotangent: bfloat16 [3, 8192, 1536], P(None, 'seq'), may hold values from -6 to 6
Outputs:
- block_out: bfloat16 [3, 8192, 1536], P(None, ('seq', 'ch'))
- input_grad: bfloat16 [3, 8192, 1536], P(None, ('seq', 'ch'))
- gain_in_grad: float32 [1536], replicated
- in_weight_grad: float32 [1536, 3, 1536], P('seq', None, 'ch')
- conv_weight_grad: float32 [3, 1536], replicated
- out_weight_grad: float32 [1536, 1536], P('seq', 'ch')
- gain_mid_grad: float32 [1536], replicated
- gate_up_grad: float32 [1536, 2, 6912], P('seq', None, 'ch')
- down_grad: float32 [1536, 6912], P('seq', 'ch')
The draws below stay inside these ranges and needn't reach their ends.
All inputs are finite; a program needn't handle non-finite values.
Results may differ from the reference program's by a relative error of at most 0.017.
Values may be sent and summed in bfloat16 or wider, within the bound.
No kernel may reach another device: no remote copies, remote signals or barrier semaphores. Data moves between devices by JAX's collectives and lax.ppermute only.
A program may use at most 320 MiB of HBM per device.

```python
import jax
import jax.numpy as jnp
from jax import lax

D = 1536
FF = 6912
KW = 3
SEQS = 3
LENGTH = 8192


def levels(rng, dims, cuts, low, high):
    level = 1.0
    for dim, shards_of in cuts:
        steps = jax.random.uniform(jax.random.fold_in(jax.random.fold_in(rng, 6), dim), (shards_of,), jnp.float32, low / len(cuts), high / len(cuts))
        level = level * jnp.repeat(jnp.exp(steps), dims[dim] // shards_of).reshape((-1,) + (1,) * (len(dims) - 1 - dim))
    return level


def normal_values(rng, shape, deviation, most, pieces=(), dtype=jnp.bfloat16):
    values = jax.random.normal(rng, shape, jnp.float32) * deviation
    if len(pieces) > 0:
        values = levels(rng, shape, pieces, -0.22, 0.18) * values
    return jnp.clip(values, min=-most, max=most).astype(dtype)


def setup_inputs(seed: int = 0) -> dict:
    key_of = jax.random.split(jax.random.key(seed), 10)
    return {
        "hidden": normal_values(key_of[0], (SEQS, LENGTH, D), 1.0, 6.0, ((1, 8),)),
        "gain_in": jnp.clip(1.0 + 0.1 * jax.random.normal(key_of[1], (D,), jnp.float32), 0.5, 1.5),
        "in_weight": normal_values(key_of[2], (D, 3, D), D ** -0.5, 0.15625, ((2, 4),)),
        "conv_weight": normal_values(key_of[3], (KW, D), 0.6, 3.0, ((1, 4),)),
        "out_weight": normal_values(key_of[4], (D, D), D ** -0.5, 0.15625, ((1, 4),)),
        "gain_mid": jnp.clip(1.0 + 0.1 * jax.random.normal(key_of[5], (D,), jnp.float32), 0.5, 1.5),
        "gate_up_weight": normal_values(key_of[6], (D, 2, FF), D ** -0.5, 0.15625, ((2, 4),)),
        "down_weight": normal_values(key_of[7], (D, FF), FF ** -0.5, 0.078125, ((1, 4),)),
        "cotangent": normal_values(key_of[8], (SEQS, LENGTH, D), 1.0, 6.0, ((1, 8),)),
    }


EPS = 1e-05
HIGH = lax.Precision.HIGHEST

@jax.custom_vjp
def low(v):
    return lax.optimization_barrier(v.astype(jnp.bfloat16)).astype(jnp.float32)

@jax.custom_vjp
def low_back(v):
    return v

def low_keep(v):
    return (low(v), None)

def low_pass(kept, grad):
    return (grad,)

def back_keep(v):
    return (v, None)

def back_low(kept, grad):
    return (low(grad),)
low.defvjp(low_keep, low_pass)
low_back.defvjp(back_keep, back_low)

def rms(rows, gain):
    return rows * lax.rsqrt(lax.optimization_barrier(jnp.mean(rows * rows, axis=-1, keepdims=True)) + EPS) * gain

def forward(rows, gain_in, w_in, w_conv, w_out, gain_mid, w_gu, w_down):
    length = rows.shape[0]
    normed = low(rms(rows, gain_in))
    proj = low_back(jnp.einsum('td,dkc->tkc', normed, w_in, precision=HIGH))
    b_gate = proj[:, 0]
    c_gate = proj[:, 1]
    x_val = proj[:, 2]
    gated = low_back(low(b_gate * x_val))
    padded = jnp.concatenate([jnp.zeros((KW - 1, D), jnp.float32), gated], axis=0)
    conv = jnp.zeros((length, D), jnp.float32)
    for tap in range(KW):
        conv = conv + w_conv[tap] * padded[tap:tap + length]
    mixed = low(c_gate * conv)
    mix_out = low_back(jnp.dot(mixed, w_out.T, precision=HIGH))
    resid = rows + mix_out
    normed2 = low(rms(resid, gain_mid))
    gate_up = low_back(jnp.einsum('td,dkf->tkf', normed2, w_gu, precision=HIGH))
    act = low(jax.nn.silu(gate_up[:, 0]) * gate_up[:, 1])
    ffn = low_back(jnp.dot(act, w_down.T, precision=HIGH))
    return resid + ffn

def reference(hidden, gain_in, in_weight, conv_weight, out_weight, gain_mid, gate_up_weight, down_weight, cotangent):
    g_in = gain_in.astype(jnp.float32)
    w_in = in_weight.astype(jnp.float32)
    w_conv = conv_weight.astype(jnp.float32)
    w_out = out_weight.astype(jnp.float32)
    g_mid = gain_mid.astype(jnp.float32)
    w_gu = gate_up_weight.astype(jnp.float32)
    w_down = down_weight.astype(jnp.float32)
    params = (g_in, w_in, w_conv, w_out, g_mid, w_gu, w_down)

    def one(totals, inputs):
        rows, grad_out = inputs
        result, pull = jax.vjp(forward, rows, g_in, w_in, w_conv, w_out, g_mid, w_gu, w_down)
        pulled = pull(grad_out)
        totals = tuple((a + b for a, b in zip(totals, pulled[1:])))
        return (totals, (result.astype(jnp.bfloat16), pulled[0].astype(jnp.bfloat16)))
    start = tuple((jnp.zeros_like(p) for p in params))
    totals, outputs = lax.scan(one, start, (hidden.astype(jnp.float32), cotangent.astype(jnp.float32)))
    return (outputs[0], outputs[1], totals[0], totals[1], totals[2], totals[3], totals[4], totals[5], totals[6])
```

```python
import jax
import jax.numpy as jnp
from jax import lax
from jax.sharding import PartitionSpec as P

EPS = 1e-05
LOW = jnp.bfloat16
CORES = 2


def norm_scale(rows):
    return lax.rsqrt(jnp.mean(rows * rows, axis=-1, keepdims=True) + EPS)


def norm_back(rows, scale, gain, grad):
    weighted = grad * gain
    inner = jnp.mean(weighted * rows, axis=-1, keepdims=True)
    d_rows = scale * weighted - rows * (scale * scale * scale) * inner
    d_gain = jnp.sum(grad * rows * scale, axis=0)
    return (d_rows, d_gain)


def dot(a, b, a_dim, b_dim):
    return lax.dot_general(
        a, b, (((a_dim,), (b_dim,)), ((), ())), preferred_element_type=jnp.float32
    )


def swap_cores(value):
    count = lax.axis_size("ch")
    return lax.ppermute(value, "ch", [(i, i ^ 1) for i in range(count)])


def shift_chips(value, steps):
    count = lax.axis_size("ch")
    return lax.ppermute(value, "ch", [(i, (i + CORES * steps) % count) for i in range(count)])


def shifted(value, axis, steps):
    count = lax.axis_size(axis)
    first, last = (max(0, -steps), min(count, count - steps))
    return lax.ppermute(value, axis, [(source, source + steps) for source in range(first, last)])


def pick(value, index):
    return lax.dynamic_index_in_dim(value, index, 0, keepdims=False)


def scatter_seq(grad):
    count = lax.axis_size("seq")
    index = lax.axis_index("seq")
    inner = 2 if count % 2 == 0 else 1
    outer = count // inner
    low, high = (index % inner, index // inner)
    rows = grad.shape[0] // count
    value = grad.reshape((outer, inner, rows) + grad.shape[1:])
    if inner == 2:
        keep = lax.dynamic_index_in_dim(value, low, 1, keepdims=False)
        give = lax.dynamic_index_in_dim(value, 1 - low, 1, keepdims=False)
        got = lax.ppermute(give, "seq", [(i, i ^ 1) for i in range(count)])
        value = (keep.astype(jnp.float32) + got.astype(jnp.float32)).astype(LOW)
    else:
        value = value[:, 0]
    ring = [(i, (i + inner) % count) for i in range(count)]
    moving = pick(value, (high + outer - 1) % outer)
    for step in range(outer - 1):
        got = lax.ppermute(moving, "seq", ring)
        total = got.astype(jnp.float32) + pick(value, (high + 2 * outer - 2 - step) % outer).astype(
            jnp.float32
        )
        moving = total if step == outer - 2 else total.astype(LOW)
    return moving.astype(jnp.float32)


def sum_all(value):
    for axis in ("ch", "seq"):
        count = lax.axis_size(axis)
        step = 1
        while step < count:
            value = value + lax.ppermute(value, axis, [(i, i ^ step) for i in range(count)])
            step *= 2
    return value


def per_device(
    hidden,
    gain_in,
    in_weight,
    conv_weight,
    out_weight,
    gain_mid,
    gate_up_weight,
    down_weight,
    cotangent,
):
    seqs, length, width = hidden.shape
    count = lax.axis_size("ch")
    chips = count // CORES
    me = lax.axis_index("ch")
    core, chip = (me % CORES, me // CORES)
    share = length // count
    taps, chans = conv_weight.shape
    hid = down_weight.shape[1]
    conv_taps = conv_weight.astype(jnp.float32)
    in_flat = in_weight.reshape(width, 3 * chans)
    out_pair = jnp.concatenate([out_weight, swap_cores(out_weight)], axis=1)
    gate_own, up_own = (gate_up_weight[:, 0], gate_up_weight[:, 1])
    gate_w = jnp.concatenate([gate_own, swap_cores(gate_own)], axis=1)
    up_w = jnp.concatenate([up_own, swap_cores(up_own)], axis=1)
    down_w = jnp.concatenate([down_weight, swap_cores(down_weight)], axis=1)
    in_other = swap_cores(in_flat)
    in_pair = jnp.concatenate([in_flat, in_other], axis=1)

    def blocks(value):
        return value.reshape((count, share) + value.shape[1:])

    order = [CORES * ((chip + k) % chips) + core for k in range(chips)]
    order_other = [CORES * ((chip + k) % chips) + (1 - core) for k in range(chips)]

    def take(value, places):
        split = blocks(value)
        return jnp.concatenate([pick(split, p) for p in places], axis=0)

    def give_rows(parts):
        return [shift_chips(parts[k], k) for k in range(1, chips)]

    def gather_rows(mine):
        return jnp.concatenate([mine] + [shift_chips(mine, -k) for k in range(1, chips)], axis=0)

    def natural(mine, other):
        both = jnp.stack(
            [
                mine.reshape((chips, share) + mine.shape[1:]),
                other.reshape((chips, share) + other.shape[1:]),
            ],
            axis=1,
        )
        both = jnp.where(core == 0, both, both[:, ::-1])
        both = jnp.concatenate([both, both], axis=0)
        both = lax.dynamic_slice_in_dim(both, (chips - chip) % chips, chips, 0)
        return both.reshape((length,) + mine.shape[1:])

    tail = shifted(hidden[:, length - (taps - 1) :], "seq", 1).reshape(seqs * (taps - 1), width)
    tail = tail.astype(jnp.float32)
    tail_normed = (tail * norm_scale(tail) * gain_in).astype(LOW)
    tail_proj = dot(tail_normed, in_flat, 1, 0)
    tail_gated = (tail_proj[:, :chans] * tail_proj[:, 2 * chans :]).astype(LOW)
    tail_gated = tail_gated.reshape(seqs, taps - 1, chans)

    kept = []
    for s in range(seqs):
        rows = hidden[s].astype(jnp.float32)
        scale_in = norm_scale(rows)
        normed = (rows * scale_in * gain_in).astype(LOW)
        proj = dot(normed, in_flat, 1, 0)
        b_gate, c_gate, x_val = (proj[:, :chans], proj[:, chans : 2 * chans], proj[:, 2 * chans :])
        gated = (b_gate * x_val).astype(LOW)
        padded = jnp.concatenate([tail_gated[s], gated], axis=0).astype(jnp.float32)
        conv = conv_taps[0] * padded[:length]
        for tap in range(1, taps):
            conv = conv + conv_taps[tap] * padded[tap : tap + length]
        mixed = (c_gate * conv).astype(LOW)
        got = swap_cores(take(mixed, order_other))
        mixed_rows = jnp.concatenate([take(mixed, order), got], axis=1)
        parts = [
            dot(mixed_rows[k * share : (k + 1) * share], out_pair, 1, 1) for k in range(chips)
        ]
        own_rows = pick(blocks(rows), me)
        resid = own_rows + parts[0]
        for part in give_rows([p.astype(LOW) for p in parts]):
            resid = resid + part.astype(jnp.float32)
        scale_mid = norm_scale(resid)
        normed_share = (resid * scale_mid * gain_mid).astype(LOW)
        normed2 = gather_rows(normed_share)
        kept.append(
            (normed, b_gate, c_gate, x_val, padded, conv, mixed_rows, own_rows, resid, scale_mid,
             normed2, pick(blocks(scale_in), me))
        )

    gain_mid_acc = jnp.zeros((width,), jnp.float32)
    gain_in_acc = jnp.zeros((width,), jnp.float32)
    conv_acc = jnp.zeros((taps, chans), jnp.float32)
    outs_rows, outs_grads, acts, d_gates, d_ups, grads, norms2 = ([], [], [], [], [], [], [])
    d_resids = []
    for s in range(seqs):
        resid, scale_mid, normed2 = (kept[s][8], kept[s][9], kept[s][10])
        grad_out = take(cotangent[s], order)
        gate_val = dot(normed2, gate_w, 1, 0)
        up_val = dot(normed2, up_w, 1, 0)
        sigm = jax.nn.sigmoid(gate_val)
        silu_val = gate_val * sigm
        act = (silu_val * up_val).astype(LOW)
        d_act = dot(grad_out, down_w, 1, 0)
        d_gate = (d_act * up_val * sigm * (1.0 + gate_val * (1.0 - sigm))).astype(LOW)
        d_up = (d_act * silu_val).astype(LOW)
        d_mid_part = dot(d_gate, gate_w, 1, 1) + dot(d_up, up_w, 1, 1)
        d_mid_parts = [d_mid_part[k * share : (k + 1) * share] for k in range(chips)]
        d_mid = d_mid_parts[0]
        for part in give_rows([p.astype(LOW) for p in d_mid_parts]):
            d_mid = d_mid + part.astype(jnp.float32)
        d_resid_norm, gain_term = norm_back(resid, scale_mid, gain_mid, d_mid)
        gain_mid_acc = gain_mid_acc + gain_term
        d_resid = grad_out[:share].astype(jnp.float32) + d_resid_norm
        d_resids.append(d_resid)
        ffn_part = dot(act, down_w, 1, 1)
        ffn = ffn_part[:share]
        for part in give_rows(
            [ffn_part[k * share : (k + 1) * share].astype(LOW) for k in range(chips)]
        ):
            ffn = ffn + part.astype(jnp.float32)
        outs_rows.append((resid + ffn).astype(LOW))
        acts.append(act)
        d_gates.append(d_gate)
        d_ups.append(d_up)
        grads.append(grad_out)
        norms2.append(normed2)

    def weight_grad(left, right, cols):
        other = swap_cores(dot(left, right[:, cols:], 0, 0).astype(LOW))
        return (dot(left, right[:, :cols], 0, 0) + other.astype(jnp.float32)).astype(LOW)

    act_all, d_gate_all, d_up_all = (
        jnp.concatenate(acts, axis=0),
        jnp.concatenate(d_gates, axis=0),
        jnp.concatenate(d_ups, axis=0),
    )
    norm2_all = jnp.concatenate(norms2, axis=0)
    down_grad = scatter_seq(weight_grad(jnp.concatenate(grads, axis=0), act_all, hid))
    gate_grad = scatter_seq(weight_grad(norm2_all, d_gate_all, hid))
    up_grad = scatter_seq(weight_grad(norm2_all, d_up_all, hid))

    d_mixes, d_projs = ([], [])
    for s in range(seqs):
        normed, b_gate, c_gate, x_val, padded, conv, mixed_rows, own_rows = kept[s][:8]
        d_resid = d_resids[s]
        d_mix = gather_rows(d_resid.astype(LOW))
        d_mixes.append(d_mix)
        d_mixed_own = dot(d_mix, out_pair[:, :chans], 1, 0)
        d_mixed_other = dot(d_mix, out_pair[:, chans:], 1, 0)
        d_mixed = natural(
            d_mixed_own.astype(LOW), swap_cores(d_mixed_other.astype(LOW))
        ).astype(jnp.float32)
        d_c = d_mixed * conv
        d_conv = d_mixed * c_gate
        d_padded = jnp.zeros((length + taps - 1, chans), jnp.float32)
        conv_terms = []
        for tap in range(taps):
            conv_terms.append(jnp.sum(d_conv * padded[tap : tap + length], axis=0))
            d_padded = d_padded + jnp.pad(conv_taps[tap] * d_conv, ((tap, taps - 1 - tap), (0, 0)))
        conv_acc = conv_acc + jnp.stack(conv_terms, axis=0)
        after = shifted(d_padded[: taps - 1], "seq", -1)
        d_gated = d_padded[taps - 1 :] + jnp.pad(after, ((length - (taps - 1), 0), (0, 0)))
        d_gated_low = d_gated.astype(LOW).astype(jnp.float32)
        d_proj = jnp.concatenate(
            [(d_gated_low * x_val).astype(LOW), d_c.astype(LOW), (d_gated_low * b_gate).astype(LOW)],
            axis=1,
        )
        d_projs.append(d_proj)
        got = swap_cores(take(d_proj, order_other))
        d_proj_rows = jnp.concatenate([take(d_proj, order), got], axis=1)
        d_in_part = dot(d_proj_rows, in_pair, 1, 1)
        d_in = d_in_part[:share]
        for part in give_rows(
            [d_in_part[k * share : (k + 1) * share].astype(LOW) for k in range(chips)]
        ):
            d_in = d_in + part.astype(jnp.float32)
        d_rows_norm, gain_term = norm_back(own_rows, kept[s][11], gain_in, d_in)
        gain_in_acc = gain_in_acc + gain_term
        outs_grads.append((d_resid + d_rows_norm).astype(LOW))

    out_grad = scatter_seq(
        weight_grad(
            jnp.concatenate(d_mixes, axis=0),
            jnp.concatenate([kept[s][6] for s in range(seqs)], axis=0),
            chans,
        )
    )
    in_grad = scatter_seq(
        dot(
            jnp.concatenate([kept[s][0] for s in range(seqs)], axis=0),
            jnp.concatenate(d_projs, axis=0),
            0,
            0,
        ).astype(LOW)
    )
    conv_full = lax.dynamic_update_slice_in_dim(
        jnp.zeros((taps, width), jnp.float32), conv_acc, me * chans, 1
    )
    small = sum_all(
        jnp.concatenate([conv_full, gain_in_acc[None], gain_mid_acc[None]], axis=0)
    )
    return (
        jnp.stack(outs_rows, axis=0),
        jnp.stack(outs_grads, axis=0),
        small[taps],
        in_grad.reshape(-1, 3, chans),
        small[:taps],
        out_grad,
        small[taps + 1],
        jnp.stack([gate_grad, up_grad], axis=1),
        down_grad,
    )


def solution(mesh):
    placed = (
        P(None, "seq", None),
        P(),
        P(None, None, "ch"),
        P(None, "ch"),
        P(None, "ch"),
        P(),
        P(None, None, "ch"),
        P(None, "ch"),
        P(None, "seq", None),
    )
    return jax.shard_map(
        per_device,
        mesh=mesh,
        in_specs=placed,
        out_specs=(
            P(None, ("seq", "ch"), None),
            P(None, ("seq", "ch"), None),
            P(),
            P("seq", None, "ch"),
            P(),
            P("seq", "ch"),
            P(),
            P("seq", None, "ch"),
            P("seq", "ch"),
        ),
        check_vma=False,
    )
```

```python
import functools

import jax
import jax.numpy as jnp
from jax import lax
from jax.experimental import pallas as pl
from jax.experimental.pallas import tpu as pltpu
from jax.sharding import PartitionSpec as P

EPS = 1e-05
LOW = jnp.bfloat16
FULL = jnp.float32
CORES = 2
HALO = 16
HIDDEN_TILE = 512
LANES = 128
ROOM = 56 << 20


def norm_scale(rows):
    return lax.rsqrt(jnp.mean(rows * rows, axis=-1, keepdims=True) + EPS)


def norm_back(rows, scale, gain, grad):
    weighted = grad * gain
    inner = jnp.mean(weighted * rows, axis=-1, keepdims=True)
    d_rows = scale * weighted - rows * (scale * scale * scale) * inner
    d_gain = jnp.sum(grad * rows * scale, axis=0)
    return (d_rows, d_gain)


def dot(a, b, a_dim, b_dim):
    return lax.dot_general(
        a, b, (((a_dim,), (b_dim,)), ((), ())), preferred_element_type=jnp.float32
    )


def swap_cores(value):
    count = lax.axis_size("ch")
    return lax.ppermute(value, "ch", [(i, i ^ 1) for i in range(count)])


def shift_chips(value, steps):
    count = lax.axis_size("ch")
    return lax.ppermute(value, "ch", [(i, (i + CORES * steps) % count) for i in range(count)])


def shifted(value, axis, steps):
    count = lax.axis_size(axis)
    first, last = (max(0, -steps), min(count, count - steps))
    return lax.ppermute(value, axis, [(source, source + steps) for source in range(first, last)])


def tie(value, *before):
    return lax.optimization_barrier((value, before))[0]


def pick(value, index):
    return lax.dynamic_index_in_dim(value, index, 0, keepdims=False)


ANY = pl.BlockSpec(memory_space=pl.ANY)


def call(kernel, name, grid, scalars, operands, outputs, scratch, carry=(), after=(), flops=0):
    extra = len(carry) + len(after)

    def body(*refs):
        place = 1 + len(operands)
        return kernel(*refs[:place], *refs[place + extra :])

    moved = sum(a.size * a.dtype.itemsize for a, _, _ in operands)
    return pl.pallas_call(
        body,
        name=name,
        grid_spec=pltpu.PrefetchScalarGridSpec(
            num_scalar_prefetch=1,
            grid=grid,
            in_specs=[pl.BlockSpec(b, m) for _, b, m in operands] + [ANY] * extra,
            out_specs=[pl.BlockSpec(b, m) for _, _, b, m in outputs],
            scratch_shapes=scratch,
        ),
        out_shape=[jax.ShapeDtypeStruct(s, d) for s, d, _, _ in outputs],
        input_output_aliases={1 + len(operands) + i: i for i in range(len(carry))},
        compiler_params=pltpu.CompilerParams(
            vmem_limit_bytes=ROOM, dimension_semantics=("arbitrary",) * len(grid)
        ),
        cost_estimate=pl.CostEstimate(flops=flops, bytes_accessed=moved, transcendentals=0),
    )(scalars, *[a for a, _, _ in operands], *carry, *after)


def conv_forward(s, scalars, hidden, tail, gain, weight, taps, carry, after):
    seqs, length, width = hidden.shape
    chans = weight.shape[2]
    kinds = weight.shape[0]
    count = lax.axis_size("ch")
    chips = count // CORES
    share = length // count
    steps = taps.shape[0]
    wide = chans % 128 == 0

    def kernel(
        at, rows_ref, halo_ref, tail_ref, gain_ref, w_ref, taps_ref,
        flip_ref, proj_ref, conv_ref, mine_ref, theirs_ref, own_ref, flat
    ):
        i = pl.program_id(0)
        if wide:
            @pl.when(i == 0)
            def _():
                for k in range(kinds):
                    flat[:, k * chans : (k + 1) * chans] = w_ref[k]

        halo = jnp.where(i == 0, tail_ref[0].astype(FULL), halo_ref[0].astype(FULL))
        rows = jnp.concatenate([halo, rows_ref[0].astype(FULL)], axis=0)
        normed = (rows * norm_scale(rows) * gain_ref[...]).astype(LOW)
        flip_ref[...] = normed[HALO:].T
        if wide:
            proj = dot(normed, flat[...], 1, 0)
            b_gate, c_gate, x_val = [proj[:, k * chans : (k + 1) * chans] for k in range(kinds)]
        else:
            b_gate, c_gate, x_val = [dot(normed, w_ref[k], 1, 0) for k in range(kinds)]
        gated = (b_gate * x_val).astype(LOW).astype(FULL)
        conv = jnp.zeros((share, chans), FULL)
        for tap in range(steps):
            back = steps - 1 - tap
            conv = conv + taps_ref[tap : tap + 1] * gated[HALO - back : HALO - back + share]
        mixed = (c_gate[HALO:] * conv).astype(LOW)
        proj_ref[0] = b_gate[HALO:].astype(LOW)
        proj_ref[1] = c_gate[HALO:].astype(LOW)
        proj_ref[2] = x_val[HALO:].astype(LOW)
        conv_ref[...] = conv.astype(LOW)

        @pl.when(i == CORES * at[0] + at[1])
        def _():
            own_ref[...] = rows_ref[0]

        @pl.when(i % CORES == at[1])
        def _():
            mine_ref[0] = mixed

        @pl.when(i % CORES != at[1])
        def _():
            theirs_ref[0] = mixed

    away = lambda i, at: ((i // CORES + chips - at[0]) % chips, 0, 0)
    return call(
        kernel,
        "conv_forward",
        (count,),
        scalars,
        [
            (hidden, (1, share, width), lambda i, at: (s, i, 0)),
            (
                hidden,
                (1, HALO, width),
                lambda i, at: (s, jnp.maximum(i * (share // HALO) - 1, 0), 0),
            ),
            (tail, (1, HALO, width), lambda i, at: (s, 0, 0)),
            (gain, (1, width), lambda i, at: (0, 0)),
            (weight, weight.shape, lambda i, at: (0, 0, 0)),
            (taps, taps.shape, lambda i, at: (0, 0)),
        ],
        [
            ((width, seqs * length), LOW, (width, share), lambda i, at: (0, s * count + i)),
            ((kinds, length, chans), LOW, (kinds, share, chans), lambda i, at: (0, i, 0)),
            ((length, chans), LOW, (share, chans), lambda i, at: (i, 0)),
            ((chips, share, chans), LOW, (1, share, chans), away),
            ((chips, share, chans), LOW, (1, share, chans), away),
            ((share, width), LOW, (share, width), lambda i, at: (0, 0)),
        ],
        [pltpu.VMEM((width, kinds * chans) if wide else (HALO, 128), LOW)],
        carry,
        after,
        2 * length * width * kinds * chans,
    )


def act_back(scalars, cotangent, downs, after):
    seqs, length, width = cotangent.shape
    hid = downs[0].shape[0]
    count = lax.axis_size("ch")
    chips = count // CORES
    share = length // count
    many = seqs * chips * share
    cols = -(-hid // LANES) * LANES
    tile = min(HIDDEN_TILE, cols)
    steps = -(-hid // tile)
    last = hid - (steps - 1) * tile
    places = [(s, k) for s in range(seqs) for k in range(chips)]

    def kernel(at, *refs):
        grad_refs, refs = refs[: len(places)], refs[len(places) :]
        down0, down1, flip, out0, out1, own, grad = refs
        i = pl.program_id(0)

        @pl.when(i == 0)
        def _():
            for n, (s, k) in enumerate(places):
                value = grad_refs[n][0]
                if k == 0:
                    own[s] = value
                grad[n * share : (n + 1) * share] = value
                flip[:, n * share : (n + 1) * share] = value.T

        def units(size):
            for down, out in ((down0, out0), (down1, out1)):
                out[:, :size] = dot(grad[...], down[:size], 1, 1).astype(LOW)

        if last == tile:
            units(tile)
        else:
            pl.when(i < steps - 1)(lambda: units(tile))
            pl.when(i == steps - 1)(lambda: units(last))

    def place(s, k):
        return lambda i, at: (s, CORES * ((at[0] + k) % chips) + at[1], 0)

    operands = [(cotangent, (1, share, width), place(s, k)) for s, k in places]
    operands += [(d, (tile, width), lambda i, at: (i, 0)) for d in downs]
    return call(
        kernel,
        "act_back",
        (steps,),
        scalars,
        operands,
        [((width, many), LOW, (width, many), lambda i, at: (0, 0))]
        + [((many, cols), LOW, (many, tile), lambda i, at: (0, i))] * 2
        + [((seqs, share, width), LOW, (seqs, share, width), lambda i, at: (0, 0, 0))],
        [pltpu.VMEM((many, width), LOW)],
        (),
        after,
        4 * many * width * hid,
    )


def ffn(s, seqs, scalars, norms, d_acts, weights, carry, after):
    chips = len(norms)
    share, width = norms[0].shape
    hid = weights[0].shape[1]
    rows = chips * share
    tile = min(HIDDEN_TILE, -(-hid // LANES) * LANES)
    steps = -(-hid // tile)
    last = hid - (steps - 1) * tile

    def kernel(at, *refs):
        norm_refs, refs = refs[:chips], refs[chips:]
        back_refs, w_refs, refs = refs[:2], refs[2:4], refs[4:]
        acts, grads, flip_n, refs = refs[:2], refs[2:4], refs[4], refs[5:]
        mid_keep, mid_give, normed, mid = refs
        i = pl.program_id(0)

        @pl.when(i == 0)
        def _():
            for k in range(chips):
                normed[k * share : (k + 1) * share] = norm_refs[k][...]
                flip_n[:, k * share : (k + 1) * share] = norm_refs[k][...].T
            mid[...] = jnp.zeros_like(mid)

        def units(size):
            for half in range(2):
                gate_w, up_w = (w_refs[half][0, :size], w_refs[half][1, :size])
                gate = dot(normed[...], gate_w, 1, 1)
                up = dot(normed[...], up_w, 1, 1)
                d_act = back_refs[half][:, :size].astype(FULL)
                sigm = jax.nn.sigmoid(gate)
                silu = gate * sigm
                act = (silu * up).astype(LOW)
                d_gate = (d_act * up * (sigm * (1.0 + gate * (1.0 - sigm)))).astype(LOW)
                d_up = (d_act * silu).astype(LOW)
                acts[half][:, :size] = act
                grads[half][0, :, :size] = d_gate
                grads[half][1, :, :size] = d_up
                mid[...] += dot(d_gate, gate_w, 1, 0) + dot(d_up, up_w, 1, 0)
                if size < tile:
                    rest = jnp.zeros((rows, tile - size), LOW)
                    acts[half][:, size:] = rest
                    grads[half][0, :, size:] = rest
                    grads[half][1, :, size:] = rest

        if last == tile:
            units(tile)
        else:
            pl.when(i < steps - 1)(lambda: units(tile))
            pl.when(i == steps - 1)(lambda: units(last))

        @pl.when(i == steps - 1)
        def _():
            mid_keep[...] = mid[:share]
            for k in range(1, chips):
                mid_give[k - 1] = mid[k * share : (k + 1) * share].astype(LOW)

    fixed = lambda i, at: (0, 0)
    operands = [(n, (share, width), fixed) for n in norms]
    operands += [(d, (rows, tile), lambda i, at: (s, i)) for d in d_acts]
    operands += [(w, (2, tile, width), lambda i, at: (0, i, 0)) for w in weights]
    many = seqs * rows
    cols = -(-hid // LANES) * LANES
    outputs = [((many, cols), LOW, (rows, tile), lambda i, at: (s, i))] * 2
    outputs += [((2, many, cols), LOW, (2, rows, tile), lambda i, at: (0, s, i))] * 2
    outputs += [((width, many), LOW, (width, rows), lambda i, at: (0, s))]
    given = (chips - 1, share, width)
    outputs += [
        ((share, width), FULL, (share, width), fixed),
        (given, LOW, given, lambda i, at: (0, 0, 0)),
    ]
    return call(
        kernel,
        "ffn",
        (steps,),
        scalars,
        operands,
        outputs,
        [
            pltpu.VMEM((rows, width), LOW),
            pltpu.VMEM((rows, width), FULL),
        ],
        carry,
        after,
        8 * rows * width * 2 * hid,
    )


def down_product(seqs, scalars, acts, downs, after):
    many, cols = acts[0].shape
    hid, width = downs[0].shape
    rows = many // seqs
    chips = lax.axis_size("ch") // CORES
    share = rows // chips
    parts = 2
    wide = width // parts

    def kernel(at, act0, act1, down0, down1, keep, give):
        value = dot(act0[:, :hid], down0[...], 1, 0) + dot(act1[:, :hid], down1[...], 1, 0)
        keep[0] = value[:share]
        for k in range(1, chips):
            give[k - 1, 0] = value[k * share : (k + 1) * share].astype(LOW)

    act_spec = ((rows, cols), lambda i, s, at: (s, 0))
    down_spec = ((hid, wide), lambda i, s, at: (0, i))
    return call(
        kernel,
        "down_product",
        (parts, seqs),
        scalars,
        [(acts[0], *act_spec), (acts[1], *act_spec), (downs[0], *down_spec), (downs[1], *down_spec)],
        [
            ((seqs, share, width), FULL, (1, share, wide), lambda i, s, at: (s, 0, i)),
            (
                (chips - 1, seqs, share, width),
                LOW,
                (chips - 1, 1, share, wide),
                lambda i, s, at: (0, s, 0, i),
            ),
        ],
        [],
        (),
        after,
        4 * many * width * hid,
    )


def weight_grad(scalars, left, right, first, kinds, other=None, bit=None, after=()):
    width, tokens = left.shape
    cols = right.shape[2]
    count = lax.axis_size("seq")
    rows = width // count
    parts = 2
    tall = width // parts
    tops = count // (2 * parts)

    def kernel(at, left_ref, right_ref, *refs):
        value = dot(left_ref[...], right_ref[0], 1, 0)
        if bit is None:
            refs[0][0] = value.astype(LOW)
            return
        if other is not None:
            value = value + refs[0][0].astype(FULL)
        value = value.astype(LOW).reshape(tops >> bit, 2, 1 << bit, rows, cols)
        zero, one = [value[:, k].reshape(tops, rows, cols) for k in range(2)]
        keep, give = refs[-2:]

        @pl.when(at[2 + bit] == 0)
        def _():
            keep[0] = zero
            give[0] = one

        @pl.when(at[2 + bit] != 0)
        def _():
            keep[0] = one
            give[0] = zero

    operands = [
        (left, (tall, tokens), lambda k, i, at: (i, 0)),
        (right, (1, tokens, cols), lambda k, i, at: (first + k, 0, 0)),
    ]
    if other is not None:
        operands.append((other, (1, tall, cols), lambda k, i, at: (first + k, i, 0)))
    if bit is not None:
        block = (1, tops, rows, cols)
        outputs = [((kinds, count // 2, rows, cols), LOW, block, lambda k, i, at: (k, i, 0, 0))] * 2
    else:
        outputs = [((kinds, width, cols), LOW, (1, tall, cols), lambda k, i, at: (k, i, 0))]
    return call(
        kernel,
        "weight_grad",
        (kinds, parts),
        scalars,
        operands,
        outputs,
        [],
        (),
        after,
        2 * kinds * width * tokens * cols,
    )


def trade(value, bit):
    count = lax.axis_size("seq")
    return lax.ppermute(value, "seq", [(i, i ^ (1 << bit)) for i in range(count)])


def total(terms):
    value = terms[0].astype(FULL)
    for term in terms[1:]:
        value = value + term.astype(FULL)
    return value


def scatter_step(terms, bits):
    bit = bits[0]
    low = sum(1 for b in bits if b < bit)
    mine = (lax.axis_index("seq") >> bit) % 2

    def half(value, which):
        split = value.reshape((-1, 2, 1 << low) + value.shape[1:])
        part = lax.dynamic_index_in_dim(split, which, 1, keepdims=False)
        return part.reshape((-1,) + value.shape[1:])

    give = total([half(t, 1 - mine) for t in terms]).astype(LOW)
    return ([half(t, mine) for t in terms] + [trade(give, bit)], give)


def conv_backward(s, seqs, scalars, mine, other, proj, conv, taps, ahead, carry, after):
    kinds, length, chans = proj.shape
    chips, share, _ = mine.shape
    count = chips * CORES
    steps = taps.shape[0]

    def kernel(
        at, mine_ref, other_ref, proj_ref, conv_ref, taps_ref, ahead_ref,
        all_ref, keep_ref, give_ref, sums_ref, later
    ):
        i = count - 1 - pl.program_id(0)

        @pl.when(pl.program_id(0) == 0)
        def _():
            later[...] = ahead_ref[...]
            sums_ref[...] = jnp.zeros_like(sums_ref)

        own = i % CORES == at[1]
        d_mixed = jnp.where(own, mine_ref[0].astype(FULL), other_ref[0].astype(FULL))
        b_gate, c_gate, x_val = [proj_ref[k].astype(FULL) for k in range(kinds)]
        gated = (b_gate * x_val).astype(LOW).astype(FULL)
        d_c = d_mixed * conv_ref[...].astype(FULL)
        d_conv = d_mixed * c_gate
        longer = jnp.concatenate([d_conv, later[...]], axis=0)
        later[...] = d_conv[:HALO]
        d_gated = jnp.zeros((share, chans), FULL)
        for tap in range(steps):
            ahead_by = steps - 1 - tap
            term = longer[ahead_by : ahead_by + share]
            d_gated = d_gated + taps_ref[tap : tap + 1] * term
            sums_ref[tap : tap + 1] += jnp.sum(term * gated, axis=0, keepdims=True)
        d_gated = d_gated.astype(LOW).astype(FULL)
        values = [(d_gated * x_val).astype(LOW), d_c.astype(LOW), (d_gated * b_gate).astype(LOW)]
        value = jnp.concatenate(values, axis=1)
        all_ref[0] = value

        @pl.when(own)
        def _():
            keep_ref[0] = value

        @pl.when(jnp.logical_not(own))
        def _():
            give_ref[0] = value

    back = lambda i: count - 1 - i
    away = lambda i, at: ((back(i) // CORES + chips - at[0]) % chips, 0, 0)
    split = ((chips, share, kinds * chans), LOW, (1, share, kinds * chans), away)
    return call(
        kernel,
        "conv_backward",
        (count,),
        scalars,
        [
            (mine, (1, share, chans), away),
            (other, (1, share, chans), away),
            (proj, (kinds, share, chans), lambda i, at: (0, back(i), 0)),
            (conv, (share, chans), lambda i, at: (back(i), 0)),
            (taps, taps.shape, lambda i, at: (0, 0)),
            (ahead, (HALO, chans), lambda i, at: (0, 0)),
        ],
        [
            (
                (1, seqs * length, kinds * chans),
                LOW,
                (1, share, kinds * chans),
                lambda i, at: (0, s * count + back(i), 0),
            ),
            split,
            split,
            ((8, chans), FULL, (8, chans), lambda i, at: (0, 0)),
        ],
        [pltpu.VMEM((HALO, chans), FULL)],
        carry,
        after,
        40 * length * chans,
    )


def per_device(
    hidden,
    gain_in,
    in_weight,
    conv_weight,
    out_weight,
    gain_mid,
    gate_up_weight,
    down_weight,
    cotangent,
):
    seqs, length, width = hidden.shape
    count = lax.axis_size("ch")
    chips = count // CORES
    me = lax.axis_index("ch")
    core, chip = (me % CORES, me // CORES)
    places = lax.axis_size("seq").bit_length() - 1
    position = lax.axis_index("seq")
    scalars = jnp.stack([chip, core] + [(position >> b) % 2 for b in range(places)])
    scalars = scalars.astype(jnp.int32)
    share = length // count
    taps, chans = conv_weight.shape
    hid = down_weight.shape[1]
    conv_taps = conv_weight.astype(FULL)

    tail = shifted(hidden[:, length - HALO :], "seq", 1)
    out_other = swap_cores(out_weight)
    in_three = jnp.transpose(in_weight, (1, 0, 2))
    gate_up = jnp.transpose(gate_up_weight, (1, 2, 0))
    down = jnp.transpose(down_weight, (1, 0))
    gate_up_other = swap_cores(gate_up)
    down_other = swap_cores(down)
    in_other = swap_cores(in_three)
    downs = (down, down_other)
    gate_ups = (gate_up, gate_up_other)
    projs, convs, mixes, owns = ([], [], [], [])
    flips = {"in": (), "grad": ()}
    arrived = {}

    def forward(s, after):
        flip, proj, conv, mine, theirs, own = conv_forward(
            s, scalars, hidden, tail, gain_in[None], in_three, conv_taps, flips["in"], after
        )
        flips["in"] = (flip,)
        projs.append(proj)
        convs.append(conv)
        owns.append(own)
        mixes.append((mine, swap_cores(theirs)))
        return (conv,)

    def mix_part(s, k, mine, got):
        return dot(mine[k], out_weight, 1, 1) + dot(got[k], out_other, 1, 1)

    def mix_send(s, after):
        mine, got = mixes[s]
        got = tie(got, after)
        sent = [mix_part(s, k, mine, got).astype(LOW) for k in range(1, chips)]
        arrived[s] = [shift_chips(p, k + 1) for k, p in enumerate(sent)]
        return tuple(sent)

    resids, scales, normed = ([], [], [])

    def join(s, after):
        mine, got = mixes[s]
        pieces = tie(arrived[s], after)
        resid = owns[s].astype(FULL) + mix_part(s, 0, mine, got)
        for piece in pieces:
            resid = resid + piece.astype(FULL)
        scale = norm_scale(resid)
        low = (resid * scale * gain_mid).astype(LOW)
        resids.append(resid)
        scales.append(scale)
        normed.append([low] + [shift_chips(low, -k) for k in range(1, chips)])
        return (low,)

    def back(after):
        flips["grad"], own, other, state["cots"] = act_back(scalars, cotangent, downs, after)
        state["d_acts"] = (own, other)
        return (own,)

    state = {
        "ffn": (),
        "proj": (),
        "conv": jnp.zeros((taps, chans), FULL),
        "in": jnp.zeros((width,), FULL),
        "mid": jnp.zeros((width,), FULL),
    }
    results, d_resids, d_mixes = ([], [], [])

    def feed(s, after):
        out = ffn(s, seqs, scalars, normed[s], state["d_acts"], gate_ups, state["ffn"], after)
        state["ffn"] = tuple(out[:5])
        keep, give = out[5:]
        results.append((keep, [shift_chips(give[k - 1], k) for k in range(1, chips)]))
        return (give,)

    def middle(s, after):
        d_mid, pieces = results[s]
        for piece in tie(pieces, after):
            d_mid = d_mid + piece.astype(FULL)
        d_norm, gain_term = norm_back(resids[s], scales[s], gain_mid, d_mid)
        d_resid = state["cots"][s].astype(FULL) + d_norm
        low = d_resid.astype(LOW)
        state["mid"] = state["mid"] + gain_term
        d_resids.append(d_resid)
        d_mixes.append([low] + [shift_chips(low, -k) for k in range(1, chips)])
        return (low,)

    mixed_backs, d_mix_rows = ([], [])

    def mix_back(s, after):
        d_mix = jnp.concatenate(tie(d_mixes[s], after), axis=0)
        d_mix_rows.append(d_mix)
        other = dot(d_mix, out_other, 1, 0).astype(LOW)
        give = swap_cores(other).reshape(chips, share, chans)
        mine = dot(d_mix, out_weight, 1, 0).astype(LOW).reshape(chips, share, chans)
        first = (chips - chip) % chips
        head = jnp.where(core == 0, pick(mine, first)[:HALO], pick(give, first)[:HALO])
        ahead = shifted(head.astype(FULL) * projs[s][1, :HALO].astype(FULL), "seq", -1)
        mixed_backs.append((mine, give, ahead))
        return (other, mine)

    proj_parts = []

    def conv_back(s, after):
        mine, give, ahead = mixed_backs[s]
        d_proj, keep, pass_on, sums = conv_backward(
            s, seqs, scalars, mine, give, projs[s], convs[s], conv_taps, ahead, state["proj"], after
        )
        state["proj"] = (d_proj,)
        state["conv"] = state["conv"] + sums[:taps]
        proj_parts.append((keep, swap_cores(pass_on)))
        return (keep,)

    in_parts = []

    def in_part(k, keep, got):
        return dot(keep[k], in_flat, 1, 1) + dot(got[k], in_flat_other, 1, 1)

    def in_send(s, after):
        keep, got = proj_parts[s]
        got = tie(got, after)
        sent = [in_part(k, keep, got).astype(LOW) for k in range(1, chips)]
        in_parts.append([shift_chips(p, k + 1) for k, p in enumerate(sent)])
        return tuple(sent)

    outs_grads = []

    def finish(s, after):
        keep, got = proj_parts[s]
        d_in = in_part(0, keep, got)
        for piece in tie(in_parts[s], after):
            d_in = d_in + piece.astype(FULL)
        rows = owns[s].astype(FULL)
        d_norm, gain_term = norm_back(rows, norm_scale(rows), gain_in, d_in)
        state["in"] = state["in"] + gain_term
        outs_grads.append((d_resids[s] + d_norm).astype(LOW))
        return (outs_grads[-1],)

    def out_send(after):
        keep, give = down_product(seqs, scalars, state["ffn"][:2], downs, after)
        state["out"] = (keep, [shift_chips(give[k - 1], k) for k in range(1, chips)])
        return (give,)

    def out_finish(after):
        keep, pieces = state["out"]
        block = jnp.stack(resids, axis=0) + keep
        for piece in tie(pieces, after):
            block = block + piece.astype(FULL)
        state["out"] = block.astype(LOW)
        return (state["out"],)

    grads = {}

    def jobs(name):
        act_own, act_other, dgu_own, dgu_other, flip_n = state["ffn"]
        if name == "down":
            return (flips["grad"], act_own[None], act_other[None])
        return (flip_n, dgu_own, dgu_other)

    def grad_other(name, kinds, after):
        left, _, other = jobs(name)
        (part,) = weight_grad(scalars, left, other, 0, kinds, after=after)
        state[name] = swap_cores(part)
        return (part,)

    def begin(name, keep, give, bits):
        grads[name] = ([keep, trade(give, bits[0])], bits[1:])

    def grad_own(name, source, kind, bits, after):
        left, own, _ = jobs(source)
        keep, give = weight_grad(scalars, left, own, kind, 1, state[source], bits[0], after)
        begin(name, keep[0], give[0], bits)
        return (keep,)

    def in_grad(bits, after):
        keep, give = weight_grad(
            scalars, flips["in"][0], state["proj"][0], 0, 1, bit=bits[0], after=after
        )
        begin("in", keep[0], give[0], bits)
        return (give,)

    def step(name, after):
        terms, bits = grads[name]
        terms, give = scatter_step(terms[:-1] + [tie(terms[-1], after)], bits)
        grads[name] = (terms, bits[1:])
        return (give,)

    def end(name, after):
        terms, bits = grads[name]
        while len(bits) > 0:
            terms, _ = scatter_step(terms, bits)
            bits = bits[1:]
        value = total(terms[:-1] + [tie(terms[-1], after)])
        grads[name] = value.reshape(value.shape[1:])
        return (grads[name],)

    def out_other_grad(after):
        other_all = jnp.concatenate([o.reshape(chips * share, chans) for _, o in mixes], axis=0)
        rows = tie(jnp.concatenate(d_mix_rows, axis=0), after)
        part = dot(rows, other_all, 0, 0).astype(LOW)
        grads["out"] = swap_cores(part)
        return (part,)

    def out_grad(bits, after):
        mine_all = jnp.concatenate([m.reshape(chips * share, chans) for m, _ in mixes], axis=0)
        rows = tie(jnp.concatenate(d_mix_rows, axis=0), after)
        value = (dot(rows, mine_all, 0, 0) + grads["out"].astype(FULL)).astype(LOW)
        value = value.reshape((lax.axis_size("seq"), -1, chans))
        terms, give = scatter_step([value], bits)
        grads["out"] = (terms, bits[1:])
        return (give,)

    def small_begin(after):
        conv_full = lax.dynamic_update_slice_in_dim(
            jnp.zeros((taps, width), FULL), state["conv"], me * chans, 1
        )
        state["small"] = jnp.concatenate(
            [conv_full, state["in"][None], state["mid"][None]], axis=0
        )
        state["hops"] = [("ch", 1 << b) for b in range(count.bit_length() - 1)]
        state["hops"] += [("seq", 1 << b) for b in range(places)]
        return after

    def small_hop(after):
        axis, flip = state["hops"].pop(0)
        pairs = [(i, i ^ flip) for i in range(lax.axis_size(axis))]
        value = tie(state["small"], after)
        state["small"] = value + lax.ppermute(value, axis, pairs)
        return after

    def flat_weights(after):
        nonlocal in_flat, in_flat_other
        in_flat = jnp.concatenate([tie(in_three, after)[k] for k in range(3)], axis=1)
        in_flat_other = jnp.concatenate([tie(in_other, after)[k] for k in range(3)], axis=1)
        return (in_flat, in_flat_other)

    in_flat = in_flat_other = None
    last = ()
    last = forward(0, last)
    last = mix_send(0, last)
    last = forward(1, last)
    last = mix_send(1, last)
    last = forward(2, last)
    last = join(0, last)
    last = mix_send(2, last)
    last = back(last)
    last = join(1, last)
    last = feed(0, last)
    last = join(2, last)
    last = feed(1, last)
    last = middle(0, last)
    last = feed(2, last)
    last = middle(1, last)
    last = mix_back(0, last)
    last = grad_other("down", 1, last)
    last = conv_back(0, last)
    last = middle(2, last)
    last = mix_back(1, last)
    last = flat_weights(last)
    last = conv_back(1, last)
    last = mix_back(2, last)
    near_y = tuple(range(places))
    near_z = (1, 0) + tuple(range(2, places))
    last = grad_own("down", "down", 0, near_y, last)
    last = grad_other("gate", 2, last)
    last = in_send(0, last)
    last = conv_back(2, last)
    last = grad_own("up", "gate", 1, near_z, last)
    last = grad_own("gate", "gate", 0, near_y, last)
    last = finish(0, last)
    last = step("down", last)
    last = in_send(1, last)
    last = in_grad(near_y, last)
    last = finish(1, last)
    last = in_send(2, last)
    last = out_other_grad(last)
    last = out_send(last)
    last = finish(2, last)
    last = step("up", last)
    last = step("gate", last)
    last = out_grad(near_y, last)
    last = step("down", last)
    last = step("in", last)
    last = small_begin(last)
    last = small_hop(last)
    last = small_hop(last)
    last = step("gate", last)
    last = end("down", last)
    last = out_finish(last)
    last = small_hop(last)
    last = step("up", last)
    last = step("in", last)
    last = end("gate", last)
    last = step("out", last)
    last = small_hop(last)
    last = step("out", last)
    last = end("up", last)
    last = end("in", last)
    last = small_hop(last)
    last = end("out", last)
    while len(state["hops"]) > 0:
        last = small_hop(last)
    down_grad, gate_grad, up_grad = [grads[n][:, :hid] for n in ("down", "gate", "up")]
    small = state["small"]
    return (
        state["out"],
        jnp.stack(outs_grads, axis=0),
        small[taps],
        grads["in"].reshape(-1, 3, chans),
        small[:taps],
        grads["out"],
        small[taps + 1],
        jnp.stack([gate_grad, up_grad], axis=1),
        down_grad,
    )


def solution(mesh):
    placed = (
        P(None, "seq", None),
        P(),
        P(None, None, "ch"),
        P(None, "ch"),
        P(None, "ch"),
        P(),
        P(None, None, "ch"),
        P(None, "ch"),
        P(None, "seq", None),
    )
    return jax.shard_map(
        per_device,
        mesh=mesh,
        in_specs=placed,
        out_specs=(
            P(None, ("seq", "ch"), None),
            P(None, ("seq", "ch"), None),
            P(),
            P("seq", None, "ch"),
            P(),
            P("seq", "ch"),
            P(),
            P("seq", None, "ch"),
            P("seq", "ch"),
        ),
        check_vma=False,
    )
```

```python
import functools

import jax
import jax.numpy as jnp
from jax import lax
from jax.experimental import pallas as pl
from jax.experimental.pallas import tpu as pltpu
from jax.sharding import PartitionSpec as P

EPS = 1e-05
LOW = jnp.bfloat16
FULL = jnp.float32
CORES = 2
HALO = 16
HIDDEN_TILE = 512
LANES = 128
COLUMN_TILE = 256
HINT = 0.5 * 1.153e9
ROOM = 56 << 20


def norm_scale(rows):
    return lax.rsqrt(jnp.mean(rows * rows, axis=-1, keepdims=True) + EPS)


def norm_back(rows, scale, gain, grad):
    weighted = grad * gain
    inner = jnp.mean(weighted * rows, axis=-1, keepdims=True)
    d_rows = scale * weighted - rows * (scale * scale * scale) * inner
    d_gain = jnp.sum(grad * rows * scale, axis=0)
    return (d_rows, d_gain)


def dot(a, b, a_dim, b_dim):
    return lax.dot_general(
        a, b, (((a_dim,), (b_dim,)), ((), ())), preferred_element_type=jnp.float32
    )


def swap_cores(value):
    count = lax.axis_size("ch")
    return lax.ppermute(value, "ch", [(i, i ^ 1) for i in range(count)])


def shift_chips(value, steps):
    count = lax.axis_size("ch")
    return lax.ppermute(value, "ch", [(i, (i + CORES * steps) % count) for i in range(count)])


def shifted(value, axis, steps):
    count = lax.axis_size(axis)
    first, last = (max(0, -steps), min(count, count - steps))
    return lax.ppermute(value, axis, [(source, source + steps) for source in range(first, last)])


def tie(value, *before):
    return lax.optimization_barrier((value, before))[0]


def pick(value, index):
    return lax.dynamic_index_in_dim(value, index, 0, keepdims=False)


ANY = pl.BlockSpec(memory_space=pl.ANY)


def call(kernel, name, grid, scalars, operands, outputs, scratch, carry=(), after=(), micros=0):
    extra = len(carry) + len(after)

    def body(*refs):
        place = 1 + len(operands)
        return kernel(*refs[:place], *refs[place + extra :])

    hint = int(micros * HINT)
    return pl.pallas_call(
        body,
        name=name,
        grid_spec=pltpu.PrefetchScalarGridSpec(
            num_scalar_prefetch=1,
            grid=grid,
            in_specs=[pl.BlockSpec(b, m) for _, b, m in operands] + [ANY] * extra,
            out_specs=[pl.BlockSpec(b, m) for _, _, b, m in outputs],
            scratch_shapes=scratch,
        ),
        out_shape=[jax.ShapeDtypeStruct(s, d) for s, d, _, _ in outputs],
        input_output_aliases={1 + len(operands) + i: i for i in range(len(carry))},
        compiler_params=pltpu.CompilerParams(
            vmem_limit_bytes=ROOM, dimension_semantics=("arbitrary",) * len(grid)
        ),
        cost_estimate=pl.CostEstimate(flops=hint, bytes_accessed=1, transcendentals=0),
    )(scalars, *[a for a, _, _ in operands], *carry, *after)


def conv_forward(s, scalars, hidden, tail, gain, weight, taps, carry, after):
    seqs, length, width = hidden.shape
    chans = weight.shape[2]
    kinds = weight.shape[0]
    count = lax.axis_size("ch")
    chips = count // CORES
    share = length // count
    steps = taps.shape[0]
    wide = chans % 128 == 0

    def kernel(
        at, rows_ref, halo_ref, tail_ref, gain_ref, w_ref, taps_ref,
        flip_ref, proj_ref, conv_ref, mine_ref, theirs_ref, own_ref, edge_ref, edge_proj, flat
    ):
        i = pl.program_id(0)
        if wide:
            @pl.when(i == 0)
            def _():
                for k in range(kinds):
                    flat[:, k * chans : (k + 1) * chans] = w_ref[k]

        halo = jnp.where(i == 0, tail_ref[0].astype(FULL), halo_ref[0].astype(FULL))
        rows = jnp.concatenate([halo, rows_ref[0].astype(FULL)], axis=0)
        normed = (rows * norm_scale(rows) * gain_ref[...]).astype(LOW)
        flip_ref[...] = normed[HALO:].T
        if wide:
            proj = dot(normed, flat[...], 1, 0)
            b_gate, c_gate, x_val = [proj[:, k * chans : (k + 1) * chans] for k in range(kinds)]
        else:
            b_gate, c_gate, x_val = [dot(normed, w_ref[k], 1, 0) for k in range(kinds)]
        gated = (b_gate * x_val).astype(LOW).astype(FULL)
        conv = jnp.zeros((share, chans), FULL)
        for tap in range(steps):
            back = steps - 1 - tap
            conv = conv + taps_ref[tap : tap + 1] * gated[HALO - back : HALO - back + share]
        mixed = (c_gate[HALO:] * conv).astype(LOW)
        proj_ref[0] = b_gate[HALO:].astype(LOW)
        proj_ref[1] = c_gate[HALO:].astype(LOW)
        proj_ref[2] = x_val[HALO:].astype(LOW)
        conv_ref[...] = conv.astype(LOW)

        @pl.when(i == 0)
        def _():
            edge_ref[...] = normed[:HALO]
            for k, value in enumerate((b_gate, c_gate, x_val)):
                edge_proj[k] = value[:HALO].astype(LOW)

        @pl.when(i == CORES * at[0] + at[1])
        def _():
            own_ref[...] = rows_ref[0]

        @pl.when(i % CORES == at[1])
        def _():
            mine_ref[0] = mixed

        @pl.when(i % CORES != at[1])
        def _():
            theirs_ref[0] = mixed

    away = lambda i, at: ((i // CORES + chips - at[0]) % chips, 0, 0)
    return call(
        kernel,
        "conv_forward",
        (count,),
        scalars,
        [
            (hidden, (1, share, width), lambda i, at: (s, i, 0)),
            (
                hidden,
                (1, HALO, width),
                lambda i, at: (s, jnp.maximum(i * (share // HALO) - 1, 0), 0),
            ),
            (tail, (1, HALO, width), lambda i, at: (s, 0, 0)),
            (gain, (1, width), lambda i, at: (0, 0)),
            (weight, weight.shape, lambda i, at: (0, 0, 0)),
            (taps, taps.shape, lambda i, at: (0, 0)),
        ],
        [
            ((width, seqs * length), LOW, (width, share), lambda i, at: (0, s * count + i)),
            ((kinds, length, chans), LOW, (kinds, share, chans), lambda i, at: (0, i, 0)),
            ((length, chans), LOW, (share, chans), lambda i, at: (i, 0)),
            ((chips, share, chans), LOW, (1, share, chans), away),
            ((chips, share, chans), LOW, (1, share, chans), away),
            ((share, width), LOW, (share, width), lambda i, at: (0, 0)),
            ((HALO, width), LOW, (HALO, width), lambda i, at: (0, 0)),
            ((kinds, HALO, chans), LOW, (kinds, HALO, chans), lambda i, at: (0, 0, 0)),
        ],
        [pltpu.VMEM((width, kinds * chans) if wide else (HALO, 128), LOW)],
        carry,
        after,
        12,
    )


def act_back(scalars, cotangent, downs, after):
    seqs, length, width = cotangent.shape
    hid = downs[0].shape[0]
    count = lax.axis_size("ch")
    chips = count // CORES
    share = length // count
    many = seqs * chips * share
    cols = -(-hid // LANES) * LANES
    tile = min(HIDDEN_TILE, cols)
    steps = -(-hid // tile)
    last = hid - (steps - 1) * tile
    places = [(s, k) for s in range(seqs) for k in range(chips)]

    def kernel(at, *refs):
        grad_refs, refs = refs[: len(places)], refs[len(places) :]
        other_refs, refs = refs[: len(places)], refs[len(places) :]
        down0, down1, flip, flip_other, out0, out1, own, grad = refs
        i = pl.program_id(0)

        @pl.when(i == 0)
        def _():
            for n, (s, k) in enumerate(places):
                value = grad_refs[n][0]
                if k == 0:
                    own[s] = value
                grad[n * share : (n + 1) * share] = value
                flip[:, n * share : (n + 1) * share] = value.T
                flip_other[:, n * share : (n + 1) * share] = other_refs[n][0].T

        def units(size):
            for down, out in ((down0, out0), (down1, out1)):
                out[:, :size] = dot(grad[...], down[:size], 1, 1).astype(LOW)

        if last == tile:
            units(tile)
        else:
            pl.when(i < steps - 1)(lambda: units(tile))
            pl.when(i == steps - 1)(lambda: units(last))

    def place(s, k, far):
        return lambda i, at: (s, CORES * ((at[0] + k) % chips) + (at[1] + far) % CORES, 0)

    operands = [
        (cotangent, (1, share, width), place(s, k, far)) for far in range(CORES) for s, k in places
    ]
    operands += [(d, (tile, width), lambda i, at: (i, 0)) for d in downs]
    return call(
        kernel,
        "act_back",
        (steps,),
        scalars,
        operands,
        [((width, many), LOW, (width, many), lambda i, at: (0, 0))] * 2
        + [((many, cols), LOW, (many, tile), lambda i, at: (0, i))] * 2
        + [((seqs, share, width), LOW, (seqs, share, width), lambda i, at: (0, 0, 0))],
        [pltpu.VMEM((many, width), LOW)],
        (),
        after,
        32,
    )


def ffn(s, seqs, scalars, norms, d_acts, weights, carry, after):
    chips = len(norms)
    share, width = norms[0].shape
    hid = weights[0].shape[1]
    rows = chips * share
    tile = min(HIDDEN_TILE, -(-hid // LANES) * LANES)
    steps = -(-hid // tile)
    last = hid - (steps - 1) * tile

    def kernel(at, *refs):
        norm_refs, refs = refs[:chips], refs[chips:]
        back_refs, w_refs, refs = refs[:2], refs[2:4], refs[4:]
        act_own, gate_own, up_own, flip_n, act_far, grad_far, flip_far, refs = refs[:7] + (refs[7:],)
        mid_keep, mid_give, normed, mid = refs
        acts = (act_own, act_far)
        gates = (gate_own, grad_far.at[0])
        ups = (up_own, grad_far.at[1])
        i = pl.program_id(0)

        @pl.when(i == 0)
        def _():
            for k in range(chips):
                normed[k * share : (k + 1) * share] = norm_refs[k][...]
                turned = norm_refs[k][...].T
                flip_n[:, k * share : (k + 1) * share] = turned
                flip_far[:, k * share : (k + 1) * share] = turned
            mid[...] = jnp.zeros_like(mid)

        def units(size):
            for half in range(2):
                gate_w, up_w = (w_refs[half][0, :size], w_refs[half][1, :size])
                gate = dot(normed[...], gate_w, 1, 1)
                up = dot(normed[...], up_w, 1, 1)
                d_act = back_refs[half][:, :size].astype(FULL)
                sigm = jax.nn.sigmoid(gate)
                silu = gate * sigm
                act = (silu * up).astype(LOW)
                d_gate = (d_act * up * (sigm * (1.0 + gate * (1.0 - sigm)))).astype(LOW)
                d_up = (d_act * silu).astype(LOW)
                acts[half][:, :size] = act
                gates[half][:, :size] = d_gate
                ups[half][:, :size] = d_up
                mid[...] += dot(d_gate, gate_w, 1, 0) + dot(d_up, up_w, 1, 0)
                if size < tile:
                    rest = jnp.zeros((rows, tile - size), LOW)
                    acts[half][:, size:] = rest
                    gates[half][:, size:] = rest
                    ups[half][:, size:] = rest

        if last == tile:
            units(tile)
        else:
            pl.when(i < steps - 1)(lambda: units(tile))
            pl.when(i == steps - 1)(lambda: units(last))

        @pl.when(i == steps - 1)
        def _():
            mid_keep[...] = mid[:share]
            for k in range(1, chips):
                mid_give[k - 1] = mid[k * share : (k + 1) * share].astype(LOW)

    fixed = lambda i, at: (0, 0)
    operands = [(n, (share, width), fixed) for n in norms]
    operands += [(d, (rows, tile), lambda i, at: (s, i)) for d in d_acts]
    operands += [(w, (2, tile, width), lambda i, at: (0, i, 0)) for w in weights]
    many = seqs * rows
    cols = -(-hid // LANES) * LANES
    outputs = [((many, cols), LOW, (rows, tile), lambda i, at: (s, i))] * 3
    outputs += [((width, many), LOW, (width, rows), lambda i, at: (0, s))]
    outputs += [((rows, cols), LOW, (rows, tile), lambda i, at: (0, i))]
    outputs += [((2, rows, cols), LOW, (2, rows, tile), lambda i, at: (0, 0, i))]
    outputs += [((width, rows), LOW, (width, rows), fixed)]
    given = (chips - 1, share, width)
    outputs += [
        ((share, width), FULL, (share, width), fixed),
        (given, LOW, given, lambda i, at: (0, 0, 0)),
    ]
    return call(
        kernel,
        "ffn",
        (steps,),
        scalars,
        operands,
        outputs,
        [
            pltpu.VMEM((rows, width), LOW),
            pltpu.VMEM((rows, width), FULL),
        ],
        carry,
        after,
        42,
    )


def down_product(scalars, act, fars, downs, after):
    rows, cols = fars[0].shape
    seqs = len(fars)
    hid, width = downs[0].shape
    chips = lax.axis_size("ch") // CORES
    share = rows // chips
    parts = 2
    wide = width // parts

    def kernel(at, act0, *refs):
        far, (down0, down1, keep, give) = refs[:seqs], refs[seqs:]
        s = pl.program_id(1)
        for n in range(seqs):

            @pl.when(s == n)
            def _():
                value = dot(act0[:, :hid], down0[...], 1, 0) + dot(far[n][:, :hid], down1[...], 1, 0)
                keep[0] = value[:share]
                for k in range(1, chips):
                    give[k - 1, 0] = value[k * share : (k + 1) * share].astype(LOW)

    down_spec = ((hid, wide), lambda i, s, at: (0, i))
    return call(
        kernel,
        "down_product",
        (parts, seqs),
        scalars,
        [(act, (rows, cols), lambda i, s, at: (s, 0))]
        + [(f, (rows, cols), lambda i, s, at: (0, 0)) for f in fars]
        + [(downs[0], *down_spec), (downs[1], *down_spec)],
        [
            ((seqs, share, width), FULL, (1, share, wide), lambda i, s, at: (s, 0, i)),
            (
                (chips - 1, seqs, share, width),
                LOW,
                (chips - 1, 1, share, wide),
                lambda i, s, at: (0, s, 0, i),
            ),
        ],
        [],
        (),
        after,
        25,
    )


def weight_grad(scalars, pairs, cuts, after):
    width = pairs[0][0].shape[0]
    cols = pairs[0][2].shape[-1]
    count = lax.axis_size("seq")
    rows = width // count
    half = count // 2

    def kernel(at, *refs):
        i = pl.program_id(0)
        value = None
        for n, (_, _, _, kind) in enumerate(pairs):
            right = refs[2 * n + 1][...] if kind is None else refs[2 * n + 1][0]
            term = dot(refs[2 * n][...], right, 1, 0)
            value = term if value is None else value + term
        value = value.astype(LOW)
        outs = refs[2 * len(pairs) :]
        for n, (bit, first, last) in enumerate(cuts):
            split = value.reshape(half >> bit, 2, 1 << bit, rows, COLUMN_TILE)
            zero, one = [split[:, k].reshape(half, rows, COLUMN_TILE) for k in range(2)]
            keep, give = outs[2 * n : 2 * n + 2]
            here = jnp.logical_and(i >= first, i < last)

            @pl.when(jnp.logical_and(here, at[2 + bit] == 0))
            def _():
                keep[...] = zero
                give[...] = one

            @pl.when(jnp.logical_and(here, at[2 + bit] != 0))
            def _():
                keep[...] = one
                give[...] = zero

    operands, outputs = ([], [])
    for left, n, right, kind in pairs:
        tokens = right.shape[-2]
        operands.append((left, (width, tokens), lambda i, at, n=n: (0, n)))
        if kind is None:
            operands.append((right, (tokens, COLUMN_TILE), lambda i, at: (0, i)))
        else:
            operands.append((right, (1, tokens, COLUMN_TILE), lambda i, at, k=kind: (k, 0, i)))

    def tile(first, last):
        return lambda i, at: (0, 0, jnp.clip(i, first, last - 1) - first)

    for _, first, last in cuts:
        wide = min(last * COLUMN_TILE, cols) - first * COLUMN_TILE
        whole = (half, rows, wide)
        outputs += [(whole, LOW, (half, rows, COLUMN_TILE), tile(first, last))] * 2
    return call(
        kernel,
        "weight_grad",
        (-(-cols // COLUMN_TILE),),
        scalars,
        operands,
        outputs,
        [],
        (),
        after,
        22 if len(pairs) > 1 else 19,
    )


def trade(value, bit):
    count = lax.axis_size("seq")
    return lax.ppermute(value, "seq", [(i, i ^ (1 << bit)) for i in range(count)])


def total(terms):
    value = terms[0].astype(FULL)
    for term in terms[1:]:
        value = value + term.astype(FULL)
    return value


def scatter_step(terms, bits):
    bit = bits[0]
    low = sum(1 for b in bits if b < bit)
    mine = (lax.axis_index("seq") >> bit) % 2

    def half(value, which):
        split = value.reshape((-1, 2, 1 << low) + value.shape[1:])
        part = lax.dynamic_index_in_dim(split, which, 1, keepdims=False)
        return part.reshape((-1,) + value.shape[1:])

    give = total([half(t, 1 - mine) for t in terms]).astype(LOW)
    return ([half(t, mine) for t in terms] + [trade(give, bit)], give)


def conv_backward(s, seqs, scalars, mine, other, proj, conv, taps, edge, carry, after):
    kinds, length, chans = proj.shape
    chips, share, _ = mine.shape
    count = chips * CORES
    steps = taps.shape[0]

    def kernel(
        at, mine_ref, other_ref, proj_ref, conv_ref, taps_ref, edge_ref,
        all_ref, keep_ref, give_ref, sums_ref, before_ref, later
    ):
        i = count - 1 - pl.program_id(0)

        @pl.when(pl.program_id(0) == 0)
        def _():
            later[...] = jnp.zeros_like(later)
            sums_ref[...] = jnp.zeros_like(sums_ref)

        own = i % CORES == at[1]
        d_mixed = jnp.where(own, mine_ref[0].astype(FULL), other_ref[0].astype(FULL))
        b_gate, c_gate, x_val = [proj_ref[k].astype(FULL) for k in range(kinds)]
        gated = (b_gate * x_val).astype(LOW).astype(FULL)
        d_c = d_mixed * conv_ref[...].astype(FULL)
        d_conv = d_mixed * c_gate
        longer = jnp.concatenate([d_conv, later[...]], axis=0)
        later[...] = d_conv[:HALO]

        def spread(longer, gated):
            size = gated.shape[0]
            d_gated = jnp.zeros((size, chans), FULL)
            for tap in range(steps):
                ahead_by = steps - 1 - tap
                term = longer[ahead_by : ahead_by + size]
                d_gated = d_gated + taps_ref[tap : tap + 1] * term
                sums_ref[tap : tap + 1] += jnp.sum(term * gated, axis=0, keepdims=True)
            return d_gated.astype(LOW).astype(FULL)

        @pl.when(i == 0)
        def _():
            b_edge, x_edge = (edge_ref[0].astype(FULL), edge_ref[2].astype(FULL))
            rows = jnp.concatenate([jnp.zeros((HALO, chans), FULL), d_conv[:HALO]], axis=0)
            d_edge = spread(rows, (b_edge * x_edge).astype(LOW).astype(FULL))
            none = jnp.zeros((HALO, chans), FULL)
            before_ref[...] = jnp.concatenate(
                [d_edge * x_edge, none, d_edge * b_edge], axis=1
            ).astype(LOW)

        d_gated = spread(longer, gated)
        values = [(d_gated * x_val).astype(LOW), d_c.astype(LOW), (d_gated * b_gate).astype(LOW)]
        value = jnp.concatenate(values, axis=1)
        all_ref[...] = value

        @pl.when(own)
        def _():
            keep_ref[0] = value

        @pl.when(jnp.logical_not(own))
        def _():
            give_ref[0] = value

    back = lambda i: count - 1 - i
    away = lambda i, at: ((back(i) // CORES + chips - at[0]) % chips, 0, 0)
    split = ((chips, share, kinds * chans), LOW, (1, share, kinds * chans), away)
    return call(
        kernel,
        "conv_backward",
        (count,),
        scalars,
        [
            (mine, (1, share, chans), away),
            (other, (1, share, chans), away),
            (proj, (kinds, share, chans), lambda i, at: (0, back(i), 0)),
            (conv, (share, chans), lambda i, at: (back(i), 0)),
            (taps, taps.shape, lambda i, at: (0, 0)),
            (edge, edge.shape, lambda i, at: (0, 0, 0)),
        ],
        [
            (
                (seqs * length, kinds * chans),
                LOW,
                (share, kinds * chans),
                lambda i, at: (s * count + back(i), 0),
            ),
            split,
            split,
            ((8, chans), FULL, (8, chans), lambda i, at: (0, 0)),
            ((HALO, kinds * chans), LOW, (HALO, kinds * chans), lambda i, at: (0, 0)),
        ],
        [pltpu.VMEM((HALO, chans), FULL)],
        carry,
        after,
        8,
    )


def per_device(
    hidden,
    gain_in,
    in_weight,
    conv_weight,
    out_weight,
    gain_mid,
    gate_up_weight,
    down_weight,
    cotangent,
):
    seqs, length, width = hidden.shape
    count = lax.axis_size("ch")
    chips = count // CORES
    me = lax.axis_index("ch")
    core, chip = (me % CORES, me // CORES)
    places = lax.axis_size("seq").bit_length() - 1
    position = lax.axis_index("seq")
    scalars = jnp.stack([chip, core] + [(position >> b) % 2 for b in range(places)])
    scalars = scalars.astype(jnp.int32)
    share = length // count
    taps, chans = conv_weight.shape
    hid = down_weight.shape[1]
    conv_taps = conv_weight.astype(FULL)

    tail = shifted(hidden[:, length - HALO :], "seq", 1)
    out_other = swap_cores(out_weight)
    in_three = jnp.transpose(in_weight, (1, 0, 2))
    gate_up = jnp.transpose(gate_up_weight, (1, 2, 0))
    down = jnp.transpose(down_weight, (1, 0))
    gate_up_other = swap_cores(gate_up)
    down_other = swap_cores(down)
    in_other = swap_cores(in_three)
    downs = (down, down_other)
    gate_ups = (gate_up, gate_up_other)
    projs, convs, mixes, owns, edges = ([], [], [], [], [])
    flips = {"in": (), "grad": ()}
    arrived = {}

    def forward(s, after):
        flip, proj, conv, mine, theirs, own, edge, edge_proj = conv_forward(
            s, scalars, hidden, tail, gain_in[None], in_three, conv_taps, flips["in"], after
        )
        flips["in"] = (flip,)
        projs.append(proj)
        convs.append(conv)
        owns.append(own)
        edges.append((edge, edge_proj))
        mixes.append((mine, swap_cores(theirs)))
        return (conv,)

    def mix_part(s, k, mine, got):
        return dot(mine[k], out_weight, 1, 1) + dot(got[k], out_other, 1, 1)

    def mix_send(s, after):
        mine, got = mixes[s]
        got = tie(got, after)
        sent = [mix_part(s, k, mine, got).astype(LOW) for k in range(1, chips)]
        arrived[s] = [shift_chips(p, k + 1) for k, p in enumerate(sent)]
        return tuple(sent)

    resids, scales, normed = ([], [], [])

    def join(s, after):
        mine, got = mixes[s]
        pieces = tie(arrived[s], after)
        resid = owns[s].astype(FULL) + mix_part(s, 0, mine, got)
        for piece in pieces:
            resid = resid + piece.astype(FULL)
        scale = norm_scale(resid)
        low = (resid * scale * gain_mid).astype(LOW)
        resids.append(resid)
        scales.append(scale)
        normed.append([low] + [shift_chips(low, -k) for k in range(1, chips)])
        return (low,)

    def back(after):
        out = act_back(scalars, cotangent, downs, after)
        flips["grad"], flips["far"], own, other, state["cots"] = out
        state["d_acts"] = (own, other)
        return (own,)

    state = {
        "ffn": (),
        "act_far": [],
        "act_sent": [],
        "grad_far": [],
        "flip_far": [],
        "proj": (),
        "conv": jnp.zeros((taps, chans), FULL),
        "in": jnp.zeros((width,), FULL),
        "mid": jnp.zeros((width,), FULL),
    }
    results, d_resids, d_mixes = ([], [], [])

    def feed(s, after):
        out = ffn(s, seqs, scalars, normed[s], state["d_acts"], gate_ups, state["ffn"], after)
        state["ffn"] = tuple(out[:4])
        act_far, grad_far, flip_far, keep, give = out[4:]
        state["act_far"].append(swap_cores(act_far))
        state["grad_far"].append(swap_cores(grad_far))
        state["flip_far"].append(swap_cores(flip_far))
        state["act_sent"].append(act_far)
        results.append((keep, [shift_chips(give[k - 1], k) for k in range(1, chips)]))
        return (give,)

    def far(s):
        return (state["act_far"][s], state["grad_far"][s], state["flip_far"][s])

    def middle(s, after):
        d_mid, pieces = results[s]
        for piece in tie(pieces, after):
            d_mid = d_mid + piece.astype(FULL)
        d_norm, gain_term = norm_back(resids[s], scales[s], gain_mid, d_mid)
        d_resid = state["cots"][s].astype(FULL) + d_norm
        low = d_resid.astype(LOW)
        state["mid"] = state["mid"] + gain_term
        d_resids.append(d_resid)
        d_mixes.append([low] + [shift_chips(low, -k) for k in range(1, chips)])
        return (low,)

    mixed_backs, d_mix_rows = ([], [])

    def mix_back(s, after):
        d_mix = jnp.concatenate(tie(d_mixes[s], after), axis=0)
        d_mix_rows.append(d_mix)
        other = dot(d_mix, out_other, 1, 0).astype(LOW)
        give = swap_cores(other).reshape(chips, share, chans)
        mine = dot(d_mix, out_weight, 1, 0).astype(LOW).reshape(chips, share, chans)
        mixed_backs.append((mine, give))
        return (other, mine)

    proj_parts, befores = ([], [])

    def conv_back(s, after):
        mine, give = mixed_backs[s]
        d_proj, keep, pass_on, sums, before = conv_backward(
            s, seqs, scalars, mine, give, projs[s], convs[s], conv_taps, edges[s][1],
            state["proj"], after,
        )
        befores.append(before)
        state["proj"] = (d_proj,)
        state["conv"] = state["conv"] + sums[:taps]
        proj_parts.append((keep, swap_cores(pass_on)))
        return (keep,)

    in_parts = []

    def in_part(k, keep, got):
        return dot(keep[k], in_flat, 1, 1) + dot(got[k], in_flat_other, 1, 1)

    def in_send(s, after):
        keep, got = proj_parts[s]
        got = tie(got, after)
        sent = [in_part(k, keep, got).astype(LOW) for k in range(1, chips)]
        in_parts.append([shift_chips(p, k + 1) for k, p in enumerate(sent)])
        return tuple(sent)

    outs_grads = []

    def arrive(s, after):
        d_in = in_part(0, *proj_parts[s])
        for piece in tie(in_parts[s], after):
            d_in = d_in + piece.astype(FULL)
        in_parts[s] = d_in
        return (d_in,)

    def finish(s, after):
        d_in = tie(in_parts[s], after).at[share - HALO :].add(state["edge"][s])
        rows = owns[s].astype(FULL)
        d_norm, gain_term = norm_back(rows, norm_scale(rows), gain_in, d_in)
        state["in"] = state["in"] + gain_term
        outs_grads.append((d_resids[s] + d_norm).astype(LOW))
        return (outs_grads[-1],)

    def out_send(after):
        keep, give = down_product(scalars, state["ffn"][0], state["act_sent"], downs, after)
        state["out"] = (keep, [shift_chips(give[k - 1], k) for k in range(1, chips)])
        return (give,)

    def out_finish(after):
        keep, pieces = state["out"]
        block = jnp.stack(resids, axis=0) + keep
        for piece in tie(pieces, after):
            block = block + piece.astype(FULL)
        state["out"] = block.astype(LOW)
        return (state["out"],)

    grads = {}

    def begin(name, keep, give, bits):
        grads[name] = ([keep, trade(give, bits[0])], bits[1:])

    def own_grad(name, pairs, orders, after):
        tiles = -(-pairs[0][2].shape[-1] // COLUMN_TILE)
        edges = [tiles * n // len(orders) for n in range(len(orders) + 1)]
        cuts = [(bits[0], edges[n], edges[n + 1]) for n, bits in enumerate(orders)]
        parts = weight_grad(scalars, pairs, cuts, after)
        for n, bits in enumerate(orders):
            begin(name + str(n), parts[2 * n], parts[2 * n + 1], bits)
        return (parts[0],)

    def down_grad(orders, after):
        pairs = [(flips["grad"], 0, state["ffn"][0], None)]
        pairs += [(flips["far"], s, state["act_far"][s], None) for s in range(seqs)]
        return own_grad("down", pairs, orders, after)

    def hidden_grad(name, kind, orders, after):
        pairs = [(state["ffn"][3], 0, state["ffn"][1 + kind], None)]
        for s in range(seqs):
            pairs.append((state["flip_far"][s], 0, state["grad_far"][s], kind))
        return own_grad(name, pairs, orders, after)

    def in_grad(orders, after):
        left = jnp.concatenate([edge for edge, _ in edges], axis=0).T
        pairs = [(flips["in"][0], 0, state["proj"][0], None)]
        pairs.append((left, 0, jnp.concatenate(befores, axis=0), None))
        return own_grad("in", pairs, orders, after)

    def edge_send(after):
        part = dot(tie(jnp.concatenate(befores, axis=0), after), in_flat, 1, 1)
        state["edge"] = shifted(part.reshape(seqs, HALO, width)[:, HALO - 8 :], "seq", -1)
        return (part,)

    def edge_hop(bit, after):
        value = tie(state["edge"], after)
        pairs = [(i, i ^ (1 << bit)) for i in range(count)]
        state["edge"] = value + lax.ppermute(value, "ch", pairs)
        return after

    def edge_place(after):
        value = jnp.pad(state["edge"], ((0, 0), (HALO - 8, 0), (0, 0)))
        state["edge"] = jnp.where(me == count - 1, value, 0.0)
        return after

    def step(name, after):
        terms, bits = grads[name]
        terms, give = scatter_step(terms[:-1] + [tie(terms[-1], after)], bits)
        grads[name] = (terms, bits[1:])
        return (give,)

    def end(name, after):
        terms, bits = grads[name]
        while len(bits) > 0:
            terms, _ = scatter_step(terms, bits)
            bits = bits[1:]
        value = total(terms[:-1] + [tie(terms[-1], after)])
        grads[name] = value.reshape(value.shape[1:])
        return (grads[name],)

    def out_other_grad(after):
        other_all = jnp.concatenate([o.reshape(chips * share, chans) for _, o in mixes], axis=0)
        rows = tie(jnp.concatenate(d_mix_rows, axis=0), after)
        part = dot(rows, other_all, 0, 0).astype(LOW)
        grads["out"] = swap_cores(part)
        return (part,)

    def out_grad(bits, after):
        mine_all = jnp.concatenate([m.reshape(chips * share, chans) for m, _ in mixes], axis=0)
        rows = tie(jnp.concatenate(d_mix_rows, axis=0), after)
        value = (dot(rows, mine_all, 0, 0) + grads["out"].astype(FULL)).astype(LOW)
        value = value.reshape((lax.axis_size("seq"), -1, chans))
        terms, give = scatter_step([value], bits)
        grads["out"] = (terms, bits[1:])
        return (give,)

    def small_begin(after):
        conv_full = lax.dynamic_update_slice_in_dim(
            jnp.zeros((taps, width), FULL), state["conv"], me * chans, 1
        )
        state["small"] = jnp.concatenate(
            [conv_full, state["in"][None], state["mid"][None]], axis=0
        )
        state["hops"] = [("ch", 1 << b) for b in range(count.bit_length() - 1)]
        state["hops"] += [("seq", 1 << b) for b in range(places)]
        return after

    def small_hop(after):
        axis, flip = state["hops"].pop(0)
        pairs = [(i, i ^ flip) for i in range(lax.axis_size(axis))]
        value = tie(state["small"], after)
        state["small"] = value + lax.ppermute(value, axis, pairs)
        return after

    def flat_weights(after):
        nonlocal in_flat, in_flat_other
        in_flat = jnp.concatenate([tie(in_three, after)[k] for k in range(3)], axis=1)
        in_flat_other = jnp.concatenate([tie(in_other, after)[k] for k in range(3)], axis=1)
        return (in_flat, in_flat_other)

    in_flat = in_flat_other = None
    near_y = tuple(range(places))
    near_z = (1, 0) + tuple(range(2, places))
    last = ()
    last = forward(0, last)
    last = mix_send(0, last)
    last = forward(1, last)
    last = mix_send(1, last)
    last = forward(2, last)
    last = join(0, last)
    last = mix_send(2, last)
    last = back(last)
    last = join(1, last)
    last = feed(0, last)
    last = join(2, last)
    last = flat_weights(last)
    last = feed(1, last)
    last = middle(0, last)
    last = feed(2, last + far(0))
    last = middle(1, last + far(1))
    last = down_grad((near_y,), last)
    last = middle(2, last)
    last = mix_back(0, last)
    last = hidden_grad("gate", 0, (near_z,), last)
    last = conv_back(0, last)
    last = mix_back(1, last)
    last = mix_back(2, last)
    last = in_send(0, last)
    last = hidden_grad("up", 1, (near_y,), last)
    last = step("down0", last)
    last = arrive(0, last)
    last = conv_back(1, last)
    last = conv_back(2, last)
    last = edge_send(last)
    last = step("gate0", last)
    last = in_send(1, last)
    last = in_send(2, last)
    last = in_grad((near_y,), last)
    last = arrive(1, last)
    last = step("down0", last)
    last = arrive(2, last)
    last = step("up0", last)
    last = out_other_grad(last)
    for bit in range(count.bit_length() - 1):
        last = edge_hop(bit, last)
    last = edge_place(last)
    last = out_send(last)
    last = out_grad(near_y, last)
    last = end("down0", last)
    last = step("gate0", last)
    last = finish(0, last)
    last = finish(1, last)
    last = finish(2, last)
    last = step("up0", last)
    last = step("in0", last)
    last = end("gate0", last)
    last = small_begin(last)
    last = small_hop(last)
    last = out_finish(last)
    last = small_hop(last)
    last = step("out", last)
    last = end("up0", last)
    last = step("in0", last)
    last = small_hop(last)
    last = step("out", last)
    last = small_hop(last)
    last = end("in0", last)
    last = small_hop(last)
    last = end("out", last)
    while len(state["hops"]) > 0:
        last = small_hop(last)

    def columns(name):
        parts = [grads[n] for n in (name + "0", name + "1") if n in grads]
        return jnp.concatenate(parts, axis=1) if len(parts) > 1 else parts[0]

    small = state["small"]
    return (
        state["out"],
        jnp.stack(outs_grads, axis=0),
        small[taps],
        columns("in").reshape(-1, 3, chans),
        small[:taps],
        grads["out"],
        small[taps + 1],
        jnp.stack([columns("gate")[:, :hid], columns("up")[:, :hid]], axis=1),
        columns("down")[:, :hid],
    )


def solution(mesh):
    placed = (
        P(None, "seq", None),
        P(),
        P(None, None, "ch"),
        P(None, "ch"),
        P(None, "ch"),
        P(),
        P(None, None, "ch"),
        P(None, "ch"),
        P(None, "seq", None),
    )
    return jax.shard_map(
        per_device,
        mesh=mesh,
        in_specs=placed,
        out_specs=(
            P(None, ("seq", "ch"), None),
            P(None, ("seq", "ch"), None),
            P(),
            P("seq", None, "ch"),
            P(),
            P("seq", "ch"),
            P(),
            P("seq", None, "ch"),
            P("seq", "ch"),
        ),
        check_vma=False,
    )
```
